32 devices in a mesh: grp: 2 (over y), neur: 16 (over z, x, core).
Axes of the slice: x: 2, y: 2, z: 4, core: 2. Of those that a mesh axis runs over, the one named last changes fastest.
Arguments:
- activations: bfloat16 [48, 3584], P('grp', 'neur'), parts along dimension 0, may hold values from -6 to 6
- residual: bfloat16 [48, 8192], P('grp'), parts along dimension 0, may hold values from -6 to 6
- down_weight: bfloat16 [3584, 8192], P('neur'), may hold values from -0.09375 to 0.09375
- norm_gain: bfloat16 [8192], replicated, may hold values from 0.5 to 1.5
- lens_weight: bfloat16 [1024, 8192], P('neur')
- targets: int32 [48], P('grp'), parts along dimension 0, may hold values from 0 to 1023
Outputs:
- attribution: float32 [48, 3584], P('grp', 'neur'), parts along dimension 0
- target_logprob: float32 [48, 20], P('grp'), parts along dimension 0
The draws below stay inside these ranges and needn't reach their ends.
There are 2 independent parts, one for each index of `grp`. The reference program is written for one: setup_inputs(seed, part) draws one part's arguments, and reference() takes and returns one part's arrays. A program takes and returns all parts, laid end to end along the dimension named above; an argument that names none is the same for every part. Nothing has to cross between parts.
All inputs are finite; a program needn't handle non-finite values.
Results may differ from the reference program's by a relative error of at most 0.007.
Values may be sent and summed in bfloat16 or wider, within the bound.
A program may use at most 64 MiB of HBM per device.

```python
import math
import jax
import jax.numpy as jnp
from jax import lax

D = 8192
PROMPTS = 24
STEPS = 20
FF = 3584
VOCAB = 1024


def draw_lens_weight(key, part):
    base_key = jax.random.fold_in(key, 0)
    unit = 4.0 / math.sqrt(D)
    drawn = jnp.clip(jax.random.normal(base_key, (VOCAB, D), jnp.float32), -6.0, 6.0)
    return (drawn * unit).astype(jnp.bfloat16)


def touch_ends(values, own_key, smallest, high):
    extent = values.shape
    index_at = [jax.random.randint(jax.random.fold_in(own_key, axis), (), 0, extent[axis]) for axis in range(len(extent))]
    values = values.at[tuple(index_at)].set(smallest)
    longest = extent.index(max(extent))
    index_at[longest] = (index_at[longest] + 1) % extent[longest]
    return values.at[tuple(index_at)].set(high)


def block_scale(rng, extent, shards, low, top_value):
    gain = 1.0
    for position, shards_of in shards:
        steps = jax.random.uniform(jax.random.fold_in(jax.random.fold_in(rng, 6), position), (shards_of,), jnp.float32, low / len(shards), top_value / len(shards))
        gain = gain * jnp.repeat(jnp.exp(steps), extent[position] // shards_of).reshape((-1,) + (1,) * (len(extent) - 1 - position))
    return gain


def bell_draw(stream_key, extent, spread, limit, shards=(), kind=jnp.bfloat16):
    array = jax.random.normal(stream_key, extent, jnp.float32) * spread
    if len(shards) > 0:
        array = block_scale(stream_key, extent, shards, -0.22, 0.18) * array
    return jnp.clip(array, min=-limit, max=limit).astype(kind)


def setup_inputs(seed: int = 0, part: int = 0) -> dict:
    keys = jax.random.split(jax.random.key(seed), 7)
    part_keys = jax.random.split(jax.random.fold_in(keys[6], part), 7)
    return {
        "activations": bell_draw(part_keys[0], (PROMPTS, FF), 1.0, 6.0, ((1, 16),)),
        "residual": bell_draw(part_keys[1], (PROMPTS, D), 1.0, 6.0),
        "down_weight": bell_draw(keys[2], (FF, D), FF ** -0.5, 0.09375, ((0, 16),)),
        "norm_gain": jnp.clip(1.0 + 0.1 * jax.random.normal(keys[3], (D,), jnp.float32), 0.5, 1.5).astype(jnp.bfloat16),
        "lens_weight": draw_lens_weight(jax.random.fold_in(keys[6], 71), part),
        "targets": touch_ends(jax.random.randint(part_keys[5], (PROMPTS,), 0, VOCAB), jax.random.fold_in(part_keys[5], 1), 0, VOCAB - 1).astype(jnp.int32),
    }


EPS = 1e-05

def reference(activations, residual, down_weight, norm_gain, lens_weight, targets):
    update = jnp.dot(activations, down_weight, preferred_element_type=jnp.float32)
    stream_base = residual.astype(jnp.float32)
    gain_vector = norm_gain.astype(jnp.float32)
    alphas = (jnp.arange(STEPS, dtype=jnp.float32) + 1.0) / STEPS

    def forward(alpha):
        stream = stream_base + alpha * update
        root_mean = jnp.sqrt(lax.optimization_barrier(jnp.mean(stream * stream, axis=1)) + EPS)
        normed = (gain_vector * stream / root_mean[:, None]).astype(jnp.bfloat16)
        logits = jnp.dot(normed, lens_weight.T, preferred_element_type=jnp.float32)
        return (logits, root_mean)
    logits, root_mean = lax.map(forward, alphas)
    row_peak = lax.optimization_barrier(jnp.max(logits, axis=2))
    exp_total = lax.optimization_barrier(jnp.sum(jnp.exp(logits - row_peak[..., None]), axis=2))
    onehot = (jnp.arange(VOCAB, dtype=jnp.int32)[None, :] == targets[:, None]).astype(jnp.float32)
    chosen = lax.optimization_barrier(jnp.sum(logits * onehot[None], axis=2))
    logprob = chosen - row_peak - jnp.log(exp_total)
    residue = onehot[None] - jnp.exp(logits - row_peak[..., None]) / exp_total[..., None]
    curvature = lax.optimization_barrier(jnp.sum(residue * logits, axis=2))
    coefficient = lax.optimization_barrier(jnp.sum(residue / root_mean[..., None], axis=0)).astype(jnp.bfloat16)
    back = jnp.dot(coefficient, lens_weight, preferred_element_type=jnp.float32)
    weight = curvature / (D * root_mean * root_mean)
    first_sum = lax.optimization_barrier(jnp.sum(weight, axis=0))
    second = lax.optimization_barrier(jnp.sum(weight * alphas[:, None], axis=0))
    grad_sum = (gain_vector * back - first_sum[:, None] * stream_base - second[:, None] * update).astype(jnp.bfloat16)
    projected = jnp.dot(grad_sum, down_weight.T, preferred_element_type=jnp.float32)
    attribution = 16.0 / STEPS * activations.astype(jnp.float32) * projected
    return (attribution, logprob.T)
```

```python
import functools

import jax
import jax.numpy as jnp
from jax import lax
from jax.experimental import pallas as pl
from jax.experimental.pallas import tpu as pltpu
from jax.sharding import PartitionSpec as P

MESH = pl.DeviceIdType.MESH
STEPS = 20
EPS = 1e-05
F32, BF16 = jnp.float32, jnp.bfloat16
LANES, GROUP = 128, 32


def nt(x, y):
    return lax.dot_general(x, y, (((1,), (1,)), ((), ())), preferred_element_type=F32)


def loop(count, body):
    if count <= 8:
        for index in range(count):
            body(index)
    else:
        pl.loop(0, count)(body)


def pack(x):
    rows, cols = x.shape
    if cols % 256 == 0:
        return jnp.concatenate([x[:, : cols // 2], x[:, cols // 2 :]], axis=0).astype(BF16)
    return jnp.concatenate([x, jnp.zeros((-rows % 16, cols), F32)], axis=0).astype(BF16)


def unpack(y, rows):
    y = y.astype(F32)
    if y.shape[0] == 2 * rows:
        return jnp.concatenate([y[:rows], y[rows:]], axis=1)
    return y[:rows]


def kernel(n, p, q, act, res, gain, tgt, down_hbm, lens_hbm, attr, logp,
           down, lens, acc, acc2, s1, r1, s2, r2, s3, r3, ug, gg, st, ebuf, mats,
           load_sem, rs_send, rs_recv, ag_send, ag_recv):
    m = p * q
    rows, width = res.shape
    vocab = lens.shape[0]
    blk = width // n
    grp, me = lax.axis_index("grp"), lax.axis_index("neur")
    core = lax.rem(me, 2)
    qi = lax.rem(me // 2, q)
    pi = me // (2 * q)
    other = 1 - core
    mine = core * m + qi * p + pi

    loads = []
    for slot, half in enumerate((other, core)):
        cols = pl.ds(pl.multiple_of(half * (width // 2), width // 2), width // 2)
        loads.append(pltpu.make_async_copy(down_hbm.at[:, cols], down.at[:, cols], load_sem.at[slot]))
    loads.append(pltpu.make_async_copy(lens_hbm, lens, load_sem.at[2]))
    for load in loads:
        load.start()

    def dev(p_at, q_at, c_at):
        return (grp, (p_at * q + q_at) * 2 + c_at)

    core_peer = dev(pi, qi, other)
    q_at = [lax.rem(qi + o, q) for o in range(1, q)]
    p_at = [lax.rem(pi + o, p) for o in range(1, p)]
    q_peers = [dev(pi, at, core) for at in q_at]
    p_peers = [dev(at, qi, core) for at in p_at]
    barrier = pltpu.get_barrier_semaphore()
    peers = [core_peer] + q_peers + p_peers
    for peer in peers:
        pl.semaphore_signal(barrier, inc=1, device_id=peer, device_id_type=MESH)
    pl.semaphore_wait(barrier, len(peers))

    sent = []

    def send(src, dst, send_sem, recv_sem, peer):
        copy = pltpu.make_async_remote_copy(
            src_ref=src, dst_ref=dst, send_sem=send_sem, recv_sem=recv_sem,
            device_id=peer, device_id_type=MESH)
        copy.start()
        sent.append(copy)
        return copy

    def cols_of(b):
        return pl.ds(pl.multiple_of(b * blk, blk), blk)

    def reduce_scatter(rd, part, before, between, filler):
        ss, rs = rs_send.at[rd], rs_recv.at[rd]

        def away(j):
            s1[rd, j] = pack(part(other * m + j))

        before()
        loop(m, away)
        first = send(s1.at[rd], r1.at[rd], ss.at[0], rs.at[0], core_peer)
        between()

        def keep(j):
            acc[j] = part(core * m + j)

        loop(m, keep)
        filler()
        first.wait_recv()

        def halved(j):
            return acc[j] + unpack(r1[rd, j], rows)

        copies = []
        for o, (at, peer) in enumerate(zip(q_at, q_peers)):
            for i in range(p):
                s2[rd, o, i] = pack(halved(at * p + i))
            copies.append(send(s2.at[rd, o], r2.at[rd, o], ss.at[1 + o], rs.at[1 + o], peer))
        for i in range(p):
            acc2[i] = halved(qi * p + i)
        for copy in copies:
            copy.wait_recv()

        def quartered(i):
            total = acc2[i]
            for o in range(q - 1):
                total = total + unpack(r2[rd, o, i], rows)
            return total

        copies = []
        for o, (at, peer) in enumerate(zip(p_at, p_peers)):
            s3[rd, o] = pack(quartered(at))
            copies.append(send(s3.at[rd, o], r3.at[rd, o], ss.at[q + o], rs.at[q + o], peer))
        total = quartered(pi)
        for copy in copies:
            copy.wait_recv()
        for o in range(p - 1):
            total = total + unpack(r3[rd, o], rows)
        return total

    def all_gather(rd, buf):
        ss, rs = ag_send.at[rd], ag_recv.at[rd]
        copies = [send(buf.at[mine], buf.at[mine], ss.at[o], rs.at[o], peer)
                  for o, peer in enumerate(p_peers)]
        for copy in copies:
            copy.wait_recv()
        part = buf.at[pl.ds(core * m + qi * p, p)]
        copies = [send(part, part, ss.at[p - 1 + o], rs.at[p - 1 + o], peer)
                  for o, peer in enumerate(q_peers)]
        for copy in copies:
            copy.wait_recv()
        part = buf.at[pl.ds(core * m, m)]
        send(part, part, ss.at[p + q - 2], rs.at[p + q - 2], core_peer).wait_recv()

    def split(x):
        high = x.astype(BF16).astype(F32)
        return jnp.concatenate([high, x - high], axis=0).astype(BF16)

    activations = act[...]

    def update_part(b):
        return jnp.dot(activations, down[:, cols_of(b)], preferred_element_type=F32)

    def lane_sum(x):
        total = x[:, :LANES]
        for at in range(LANES, x.shape[1], LANES):
            total = total + x[:, at : at + LANES]
        return total

    mats[...] = jnp.zeros_like(mats)
    acc_a, acc_b = mats.at[0], mats.at[1]
    sq_rr, sq_ru, sq_uu = (mats.at[2 + i, pl.ds(0, rows)] for i in range(3))

    def residual_terms():
        loads[2].wait()

        def body(b):
            base = res[:, cols_of(b)].astype(F32)
            sq_rr[...] += lane_sum(base * base)
            acc_a[:, :vocab] += nt(split(gain[:, cols_of(b)] * base), lens[:, cols_of(b)])

        loop(n, body)

    with jax.named_scope("update_sum"):
        update = reduce_scatter(0, update_part, loads[0].wait, loads[1].wait, residual_terms)
    ug[mine] = pack(update)
    with jax.named_scope("update_gather"):
        all_gather(0, ug)

    def update_terms(b):
        base = res[:, cols_of(b)].astype(F32)
        up = unpack(ug[b], rows)
        sq_ru[...] += lane_sum(base * up)
        sq_uu[...] += lane_sum(up * up)
        acc_b[:, :vocab] += nt(split(gain[:, cols_of(b)] * up), lens[:, cols_of(b)])

    loop(n, update_terms)

    with jax.named_scope("softmax_parts"):
        a_log = acc_a[:rows, :vocab] + acc_a[rows:, :vocab]
        b_log = acc_b[:rows, :vocab] + acc_b[rows:, :vocab]
        rr = jnp.sum(sq_rr[...], axis=1, keepdims=True) * (1.0 / width)
        ru = jnp.sum(sq_ru[...], axis=1, keepdims=True) * (2.0 / width)
        uu = jnp.sum(sq_uu[...], axis=1, keepdims=True) * (1.0 / width)
        lane = lax.broadcasted_iota(jnp.int32, (rows, LANES), 1)
        alphas = (lane + 1).astype(F32) / STEPS
        live = lane < STEPS
        inv_root = 1.0 / jnp.sqrt(rr + alphas * ru + alphas * alphas * uu + EPS)
        inv_root = jnp.where(live, inv_root, 0.0)
        hit = lax.broadcasted_iota(jnp.int32, (rows, vocab), 1) + me * vocab == tgt[...]
        a_hit = jnp.sum(jnp.where(hit, a_log, 0.0), axis=1, keepdims=True)
        b_hit = jnp.sum(jnp.where(hit, b_log, 0.0), axis=1, keepdims=True)
        chosen = (a_hit + alphas * b_hit) * inv_root
        peaks = jnp.zeros((rows, LANES), F32)
        packed = pltpu.roll(chosen, 3 * GROUP, 1)
        for k in range(STEPS):
            logits = (a_log + ((k + 1) / STEPS) * b_log) * inv_root[:, k : k + 1]
            peak = jnp.max(logits, axis=1, keepdims=True)
            grown = jnp.exp(logits - peak)
            ebuf[k] = grown
            peaks = jnp.where(lane == k, peak, peaks)
            packed = jnp.where(lane == GROUP + k, jnp.sum(grown, axis=1, keepdims=True), packed)
            packed = jnp.where(lane == 2 * GROUP + k, jnp.sum(grown * logits, axis=1, keepdims=True), packed)
        st[mine] = jnp.where(lane < GROUP, peaks, packed)
    with jax.named_scope("softmax_gather"):
        all_gather(1, st)

    with jax.named_scope("softmax_whole"):
        top = st[0]
        for b in range(1, n):
            top = jnp.maximum(top, st[b])
        total = jnp.zeros((rows, LANES), F32)
        moment = jnp.zeros((rows, LANES), F32)
        plain = jnp.zeros((rows, LANES), F32)
        for b in range(n):
            x = st[b]
            factor = jnp.exp(x - top)
            total += factor * pltpu.roll(x, 3 * GROUP, 1)
            moment += factor * pltpu.roll(x, 2 * GROUP, 1)
            plain += x
        total = jnp.where(live, total, 1.0)
        chosen = pltpu.roll(plain, GROUP, 1)
        logp[...] = (chosen - top - jnp.log(total))[:, :STEPS]
        weight = (chosen - moment / total) * inv_root * inv_root * (1.0 / width)
        weight = jnp.where(live, weight, 0.0)
        first_sum = jnp.sum(weight, axis=1, keepdims=True)
        second_sum = jnp.sum(weight * alphas, axis=1, keepdims=True)
        scale = jnp.where(live, jnp.exp(peaks - top), 0.0) / total * inv_root
        coefficient = jnp.where(hit, jnp.sum(inv_root, axis=1, keepdims=True), 0.0)
        for k in range(STEPS):
            coefficient = coefficient - ebuf[k] * scale[:, k : k + 1]
        coefficient = coefficient.astype(BF16)

    def back_part(b):
        return jnp.dot(coefficient, lens[:, cols_of(b)], preferred_element_type=F32)

    def nothing():
        return None

    with jax.named_scope("back_sum"):
        back = reduce_scatter(1, back_part, nothing, nothing, nothing)
    own = cols_of(mine)
    gg[mine] = pack(gain[:, own] * back - first_sum * res[:, own].astype(F32) - second_sum * update)
    with jax.named_scope("gradient_gather"):
        all_gather(2, gg)

    with jax.named_scope("projection"):
        folds = gg.shape[1] // rows
        step = gg.shape[2]
        neurons = down.shape[0]
        proj = jnp.zeros((rows, neurons), F32)
        for b in range(n):
            for f in range(folds):
                at = b * blk + f * step
                proj += nt(gg[b], down[:, at : at + step])[f * rows : (f + 1) * rows]
        attr[...] = 16.0 / STEPS * activations.astype(F32) * proj
    for copy in sent:
        copy.wait_send()


def solution(mesh):
    n = mesh.shape["neur"]
    p, q = 4, n // 8
    m = p * q

    def local(activations, residual, down_weight, norm_gain, lens_weight, targets):
        rows, width = residual.shape
        neurons, vocab = down_weight.shape[0], lens_weight.shape[0]
        blk = width // n
        piece = (2 * rows, blk // 2) if blk % 256 == 0 else (rows + -rows % 16, blk)
        vmem, hbm = pl.BlockSpec(memory_space=pltpu.VMEM), pl.BlockSpec(memory_space=pl.ANY)
        sem = pltpu.SemaphoreType.DMA
        return pl.pallas_call(
            functools.partial(kernel, n, p, q),
            out_shape=(
                jax.ShapeDtypeStruct((rows, neurons), F32),
                jax.ShapeDtypeStruct((rows, STEPS), F32),
            ),
            in_specs=[vmem, vmem, vmem, vmem, hbm, hbm],
            out_specs=(vmem, vmem),
            scratch_shapes=[
                pltpu.VMEM(down_weight.shape, BF16),
                pltpu.VMEM(lens_weight.shape, BF16),
                pltpu.VMEM((m, rows, blk), F32),
                pltpu.VMEM((p, rows, blk), F32),
                pltpu.VMEM((2, m) + piece, BF16),
                pltpu.VMEM((2, m) + piece, BF16),
                pltpu.VMEM((2, q - 1, p) + piece, BF16),
                pltpu.VMEM((2, q - 1, p) + piece, BF16),
                pltpu.VMEM((2, p - 1) + piece, BF16),
                pltpu.VMEM((2, p - 1) + piece, BF16),
                pltpu.VMEM((n,) + piece, BF16),
                pltpu.VMEM((n,) + piece, BF16),
                pltpu.VMEM((n, rows, LANES), F32),
                pltpu.VMEM((STEPS, rows, vocab), F32),
                pltpu.VMEM((5, 2 * rows, LANES), F32),
                sem((3,)),
                sem((2, p + q - 1)),
                sem((2, p + q - 1)),
                sem((3, p + q - 1)),
                sem((3, p + q - 1)),
            ],
            compiler_params=pltpu.CompilerParams(
                collective_id=0, has_side_effects=True, vmem_limit_bytes=40 * 1024 * 1024
            ),
        )(activations, residual, norm_gain.astype(F32).reshape(1, width), targets.reshape(rows, 1),
          down_weight, lens_weight)

    placed = (P("grp", "neur"), P("grp", None), P("neur", None), P(), P("neur", None), P("grp"))
    return jax.shard_map(
        local,
        mesh=mesh,
        in_specs=placed,
        out_specs=(P("grp", "neur"), P("grp", None)),
        check_vma=False,
    )
```

```python
import functools

import jax
import jax.numpy as jnp
from jax import lax
from jax.experimental import pallas as pl
from jax.experimental.pallas import tpu as pltpu
from jax.sharding import PartitionSpec as P

MESH = pl.DeviceIdType.MESH
STEPS = 20
EPS = 1e-05
F32, BF16 = jnp.float32, jnp.bfloat16
LANES = 128


def nt(x, y):
    return lax.dot_general(x, y, (((1,), (1,)), ((), ())), preferred_element_type=F32)


def loop(count, body):
    if count <= 8:
        for index in range(count):
            body(index)
    else:
        pl.loop(0, count)(body)


def pack(x):
    rows, cols = x.shape
    if cols % 256 == 0:
        return jnp.concatenate([x[:, : cols // 2], x[:, cols // 2 :]], axis=0).astype(BF16)
    return jnp.concatenate([x, jnp.zeros((-rows % 16, cols), F32)], axis=0).astype(BF16)


def unpack(y, rows):
    y = y.astype(F32)
    if y.shape[0] == 2 * rows:
        return jnp.concatenate([y[:rows], y[rows:]], axis=1)
    return y[:rows]


def fold(x):
    lane = lax.broadcasted_iota(jnp.int32, (8, LANES), 1)
    first = jnp.where(lane < LANES // 2, x[:8], pltpu.roll(x[8:16], LANES // 2, 1))
    return jnp.concatenate([first, x[16:24]], axis=0)


def unfold(y):
    return jnp.concatenate([y[:8], pltpu.roll(y[:8], LANES // 2, 1), y[8:16]], axis=0)


def kernel(n, chunks, act_hbm, res_hbm, gain_hbm, tgt_hbm, down_hbm, lens_hbm, attr, logp,
           act, res, rawgain, gain, tgt, down, lens, acc, s1, r1, s2, r2, ug, gg, st, part_s, part_r,
           ebuf, mats, projected, load_sem, rs_send, rs_recv, ag_send, ag_recv, pair_send, pair_recv):
    m = n // 2
    q = n // 8
    p = m // q
    rows, half = res.shape
    width = 2 * half
    vocab = 2 * lens.shape[1]
    span = half // chunks
    blk = span // m
    grp, me = lax.axis_index("grp"), lax.axis_index("neur")
    core = lax.rem(me, 2)
    spot = lax.rem(me // 2, q) * p + me // (2 * q)
    other = 1 - core

    def half_of(c):
        return pl.ds(pl.multiple_of(c * half, half), half)

    loads = [pltpu.make_async_copy(act_hbm, act, load_sem.at[0])]
    for slot in range(2 * chunks):
        at = (other, core)[slot // chunks] * half + (slot % chunks) * span
        cols = pl.ds(pl.multiple_of(at, span), span)
        loads.append(pltpu.make_async_copy(down_hbm.at[:, cols], down.at[:, cols], load_sem.at[1 + slot]))
    for slot, (src, dst) in enumerate(((lens_hbm.at[:, half_of(core)], lens.at[core]), (res_hbm.at[:, half_of(core)], res),
                                       (gain_hbm, rawgain), (tgt_hbm, tgt))):
        loads.append(pltpu.make_async_copy(src, dst, load_sem.at[1 + 2 * chunks + slot]))
    for load in loads:
        load.start()

    def dev(spot_at, c_at):
        return (grp, (lax.rem(spot_at, p) * q + spot_at // p) * 2 + c_at)

    core_peer = dev(spot, other)
    ahead = [lax.rem(spot + o, m) for o in range(m)]
    behind = [lax.rem(spot + m - o, m) for o in range(m)]
    barrier = pltpu.get_barrier_semaphore()
    for peer in [core_peer] + [dev(at, core) for at in ahead[1:]]:
        pl.semaphore_signal(barrier, inc=1, device_id=peer, device_id_type=MESH)
    pl.semaphore_wait(barrier, m)

    sent = []

    def send(src, dst, send_sem, recv_sem, peer):
        copy = pltpu.make_async_remote_copy(
            src_ref=src, dst_ref=dst, send_sem=send_sem, recv_sem=recv_sem,
            device_id=peer, device_id_type=MESH)
        copy.start()
        sent.append(copy)
        return copy

    heads = send(lens_hbm.at[:, half_of(other)], lens.at[core], pair_send.at[0], pair_recv.at[0], core_peer)

    def cols_of(c, j):
        return pl.ds(pl.multiple_of(c * span + j * blk, blk), blk)

    def send_sums(rd, c, part):
        ss, rs = rs_send.at[rd, c], rs_recv.at[rd, c]
        copies = []
        for o in range(1, m):
            s2[rd, c, o - 1] = pack(part(ahead[o]))
            copies.append(send(s2.at[rd, c, o - 1], r2.at[rd, c, o - 1], ss.at[o], rs.at[o], dev(ahead[o], core)))
        return copies

    def take_sums(rd, c, copies, total):
        for o in range(1, m):
            copies[o - 1].wait_recv()
            total = total + unpack(r2[rd, c, o - 1], rows)
        return total

    def gather(rd, c, own):
        ss, rs = ag_send.at[rd, c], ag_recv.at[rd, c]
        return [send(own, own, ss.at[o], rs.at[o], dev(ahead[o], core)) for o in range(1, m)]

    def split(x):
        high = x.astype(BF16).astype(F32)
        return jnp.concatenate([high, x - high], axis=0).astype(BF16)

    loads[0].wait()
    activations = act[...]

    def lane_sum(x):
        total = x[:, :LANES]
        for at in range(LANES, x.shape[1], LANES):
            total = total + x[:, at : at + LANES]
        return total

    def head(c):
        return lens[:, :, c * span : (c + 1) * span].reshape(vocab, span)

    def joined(buf, c, base):
        return jnp.concatenate([unpack(buf[c, base + j], rows) for j in range(m)], axis=1)

    mats[...] = jnp.zeros_like(mats)
    projected[...] = jnp.zeros_like(projected)
    acc_a, acc_b = mats.at[0], mats.at[1]
    sq_rr, sq_ru, sq_uu = (mats.at[2 + i, pl.ds(0, rows)] for i in range(3))

    def residual_terms():
        for load in loads[1 + 2 * chunks :]:
            load.wait()
        heads.wait_recv()
        mine = rawgain[core].astype(F32)
        for at in range(half // LANES):
            gain[:, at * LANES : (at + 1) * LANES] = mine[at : at + 1, :]
        for c in range(chunks):
            cols = slice(c * span, (c + 1) * span)
            base = res[:, cols].astype(F32)
            sq_rr[...] += lane_sum(base * base)
            acc_a[:, :vocab] += nt(split(gain[:, cols] * base), head(c))

    with jax.named_scope("update_sum"):
        def product(c, at, j):
            cols = pl.ds(pl.multiple_of(at * half + c * span + j * blk, blk), blk)
            return jnp.dot(activations, down[:, cols], preferred_element_type=F32)

        firsts = []
        for c in range(chunks):
            loads[1 + c].wait()
            for j in range(m):
                s1[c, j] = pack(product(c, other, j))
            firsts.append(send(s1.at[c], r1.at[c], pair_send.at[2 + c], pair_recv.at[2 + c], core_peer))
        for c in range(chunks):
            loads[1 + chunks + c].wait()
            for j in range(m):
                acc[c, j] = product(c, core, j)

        sums = []
        for c in range(chunks):
            firsts[c].wait_recv()

            def halved(j):
                return acc[c, j] + unpack(r1[c, j], rows)

            sums.append((send_sums(0, c, halved), halved(spot)))
        residual_terms()

    with jax.named_scope("update_gather"):
        updates, gathers = [], []
        for c in range(chunks):
            updates.append(take_sums(0, c, *sums[c]))
            ug[c, spot] = pack(updates[c])
            gathers.append(gather(0, c, ug.at[c, spot]))
        for c in range(chunks):
            for copy in gathers[c]:
                copy.wait_recv()
            cols = slice(c * span, (c + 1) * span)
            up = joined(ug, c, 0)
            sq_ru[...] += lane_sum(res[:, cols].astype(F32) * up)
            sq_uu[...] += lane_sum(up * up)
            acc_b[:, :vocab] += nt(split(gain[:, cols] * up), head(c))

    with jax.named_scope("pair_sum"):
        lane = lax.broadcasted_iota(jnp.int32, (rows, LANES), 1)
        part_s[0] = acc_a[:rows, :] + acc_a[rows:, :]
        part_s[1] = acc_b[:rows, :] + acc_b[rows:, :]
        norms = jnp.zeros((rows, LANES), F32)
        for i, sq in enumerate((sq_rr, sq_ru, sq_uu)):
            norms = jnp.where(lane == i, jnp.sum(sq[...], axis=1, keepdims=True), norms)
        part_s[2] = norms
        send(part_s, part_r, pair_send.at[1], pair_recv.at[1], core_peer).wait_recv()

    with jax.named_scope("softmax_parts"):
        a_log = (part_s[0] + part_r[0])[:, :vocab]
        b_log = (part_s[1] + part_r[1])[:, :vocab]
        norms = part_s[2] + part_r[2]
        rr = norms[:, 0:1] * (1.0 / width)
        ru = norms[:, 1:2] * (2.0 / width)
        uu = norms[:, 2:3] * (1.0 / width)
        alphas = (lane + 1).astype(F32) / STEPS
        live = lane < STEPS
        inv_root = 1.0 / jnp.sqrt(rr + alphas * ru + alphas * alphas * uu + EPS)
        inv_root = jnp.where(live, inv_root, 0.0)
        square = lax.broadcasted_iota(jnp.int32, (rows, rows), 0) == lax.broadcasted_iota(jnp.int32, (rows, rows), 1)
        target = jnp.sum(jnp.where(square, tgt[...].astype(F32), 0.0), axis=1, keepdims=True).astype(jnp.int32)
        hit = lax.broadcasted_iota(jnp.int32, (rows, vocab), 1) + (me // 2) * vocab == target
        a_hit = jnp.sum(jnp.where(hit, a_log, 0.0), axis=1, keepdims=True)
        b_hit = jnp.sum(jnp.where(hit, b_log, 0.0), axis=1, keepdims=True)
        peaks = jnp.zeros((rows, LANES), F32)
        packed = jnp.where(lane == 3 * STEPS, a_hit, jnp.where(lane == 3 * STEPS + 1, b_hit, 0.0))
        for k in range(STEPS):
            logits = (a_log + ((k + 1) / STEPS) * b_log) * inv_root[:, k : k + 1]
            peak = jnp.max(logits, axis=1, keepdims=True)
            grown = jnp.exp(logits - peak)
            ebuf[k] = grown
            peaks = jnp.where(lane == k, peak, peaks)
            packed = jnp.where(lane == STEPS + k, jnp.sum(grown, axis=1, keepdims=True), packed)
            packed = jnp.where(lane == 2 * STEPS + k, jnp.sum(grown * logits, axis=1, keepdims=True), packed)
        st[spot] = fold(jnp.where(live, peaks, packed))
    with jax.named_scope("softmax_gather"):
        for copy in gather(1, 0, st.at[spot]):
            copy.wait_recv()

    with jax.named_scope("softmax_whole"):
        top = st[0]
        for j in range(1, m):
            top = jnp.maximum(top, st[j])
        total, moment, plain = (jnp.zeros(top.shape, F32) for _ in range(3))
        for j in range(m):
            x = st[j]
            factor = jnp.exp(x - top)
            total += factor * pltpu.roll(x, LANES - STEPS, 1)
            moment += factor * pltpu.roll(x, LANES - 2 * STEPS, 1)
            plain += x
        top, total, moment, plain = unfold(top), unfold(total), unfold(moment), unfold(plain)
        total = jnp.where(live, total, 1.0)
        chosen = (plain[:, 3 * STEPS : 3 * STEPS + 1] + alphas * plain[:, 3 * STEPS + 1 : 3 * STEPS + 2]) * inv_root
        logp[...] = (chosen - top - jnp.log(total))[:, :STEPS]
        weight = (chosen - moment / total) * inv_root * inv_root * (1.0 / width)
        weight = jnp.where(live, weight, 0.0)
        first_sum = jnp.sum(weight, axis=1, keepdims=True)
        second_sum = jnp.sum(weight * alphas, axis=1, keepdims=True)
        scale = jnp.where(live, jnp.exp(peaks - top), 0.0) / total * inv_root
        coefficient = jnp.where(hit, jnp.sum(inv_root, axis=1, keepdims=True), 0.0)
        for k in range(STEPS):
            coefficient = coefficient - ebuf[k] * scale[:, k : k + 1]
        coefficient = coefficient.astype(BF16)

    with jax.named_scope("back_sum"):
        sums = []
        for c in range(chunks):
            def back_part(j):
                block = lens[:, :, cols_of(c, j)].reshape(vocab, blk)
                return jnp.dot(coefficient, block, preferred_element_type=F32)

            sums.append((send_sums(1, c, back_part), back_part(spot)))

    with jax.named_scope("gradient_gather"):
        gathers, relays = [], []

        def relay(c, j, slot):
            block = gg.at[c, core * m + j]
            relays[c].append(send(block, block, ag_send.at[2, c, slot], ag_recv.at[2, c, slot], core_peer))

        for c in range(chunks):
            back = take_sums(1, c, *sums[c])
            own = cols_of(c, spot)
            gg[c, core * m + spot] = pack(
                gain[:, own] * back - first_sum * res[:, own].astype(F32) - second_sum * updates[c])
            gathers.append(gather(2, c, gg.at[c, core * m + spot]))
            relays.append([])
            relay(c, spot, m)

        def project(c, at):
            cols = pl.ds(pl.multiple_of(at * half + c * span, span), span)
            projected[...] += nt(joined(gg, c, at * m).astype(BF16), down[:, cols])

        for c in range(chunks):
            for o in range(1, m):
                gathers[c][o - 1].wait_recv()
                relay(c, behind[o], m + o)
            project(c, core)
            for copy in relays[c]:
                copy.wait_recv()
            project(c, other)
    attr[...] = 16.0 / STEPS * activations.astype(F32) * projected[...]
    for copy in sent:
        copy.wait_send()


def solution(mesh):
    n = mesh.shape["neur"]
    m = n // 2

    def local(activations, residual, down_weight, norm_gain, lens_weight, targets):
        rows, width = residual.shape
        neurons, vocab = down_weight.shape[0], lens_weight.shape[0]
        chunks = 2 if width // n % 512 == 0 else 1
        blk = width // n // chunks
        piece = (2 * rows, blk // 2) if blk % 256 == 0 else (rows + -rows % 16, blk)
        vmem, hbm = pl.BlockSpec(memory_space=pltpu.VMEM), pl.BlockSpec(memory_space=pltpu.HBM)
        sem = pltpu.SemaphoreType.DMA
        half = width // 2
        gains = (2, half // LANES, LANES)
        return pl.pallas_call(
            functools.partial(kernel, n, chunks),
            out_shape=(
                jax.ShapeDtypeStruct((rows, neurons), F32),
                jax.ShapeDtypeStruct((rows, STEPS), F32),
            ),
            in_specs=[hbm] * 6,
            out_specs=(vmem, vmem),
            scratch_shapes=[
                pltpu.VMEM(activations.shape, BF16),
                pltpu.VMEM((rows, half), BF16),
                pltpu.VMEM(gains, BF16),
                pltpu.VMEM((1, half), F32),
                pltpu.VMEM((1, rows), jnp.int32),
                pltpu.VMEM(down_weight.shape, BF16),
                pltpu.VMEM((2, vocab, half), BF16),
                pltpu.VMEM((chunks, m, rows, blk), F32),
                pltpu.VMEM((chunks, m) + piece, BF16),
                pltpu.VMEM((chunks, m) + piece, BF16),
                pltpu.VMEM((2, chunks, m - 1) + piece, BF16),
                pltpu.VMEM((2, chunks, m - 1) + piece, BF16),
                pltpu.VMEM((chunks, m) + piece, BF16),
                pltpu.VMEM((chunks, n) + piece, BF16),
                pltpu.VMEM((m, 16, LANES), F32),
                pltpu.VMEM((3, rows, LANES), F32),
                pltpu.VMEM((3, rows, LANES), F32),
                pltpu.VMEM((STEPS, rows, 2 * vocab), F32),
                pltpu.VMEM((5, 2 * rows, LANES), F32),
                pltpu.VMEM((rows, neurons), F32),
                sem((5 + 2 * chunks,)),
                sem((2, chunks, m)),
                sem((2, chunks, m)),
                sem((3, chunks, n)),
                sem((3, chunks, n)),
                sem((2 + chunks,)),
                sem((2 + chunks,)),
            ],
            compiler_params=pltpu.CompilerParams(
                collective_id=0, has_side_effects=True, vmem_limit_bytes=40 * 1024 * 1024
            ),
        )(*[pltpu.with_memory_space_constraint(x, pltpu.HBM) for x in (activations, residual, norm_gain.reshape(gains), targets.reshape(1, rows), down_weight, lens_weight)])

    placed = (P("grp", "neur"), P("grp", None), P("neur", None), P(), P("neur", None), P("grp"))
    return jax.shard_map(
        local,
        mesh=mesh,
        in_specs=placed,
        out_specs=(P("grp", "neur"), P("grp", None)),
        check_vma=False,
    )
```

```python
import functools

import jax
import jax.numpy as jnp
from jax import lax
from jax.experimental import pallas as pl
from jax.experimental.pallas import tpu as pltpu
from jax.sharding import PartitionSpec as P

MESH = pl.DeviceIdType.MESH
STEPS = 20
EPS = 1e-05
F32, BF16 = jnp.float32, jnp.bfloat16
LANES = 128


def nt(x, y):
    return lax.dot_general(x, y, (((1,), (1,)), ((), ())), preferred_element_type=F32)


def pack(x):
    rows, cols = x.shape
    if cols % 256 == 0:
        return jnp.concatenate([x[:, : cols // 2], x[:, cols // 2 :]], axis=0).astype(BF16)
    return jnp.concatenate([x, jnp.zeros((-rows % 16, cols), F32)], axis=0).astype(BF16)


def unpack(y, rows):
    y = y.astype(F32)
    if y.shape[0] == 2 * rows:
        return jnp.concatenate([y[:rows], y[rows:]], axis=1)
    return y[:rows]


def fold(x):
    lane = lax.broadcasted_iota(jnp.int32, (8, LANES), 1)
    first = jnp.where(lane < LANES // 2, x[:8], pltpu.roll(x[8:16], LANES // 2, 1))
    return jnp.concatenate([first, x[16:24]], axis=0)


def unfold(y):
    return jnp.concatenate([y[:8], pltpu.roll(y[:8], LANES // 2, 1), y[8:16]], axis=0)


def kernel(n, chunks, act_hbm, res_hbm, gain_hbm, tgt_hbm, down_hbm, lens_hbm, attr, logp,
           act, res, rawgain, gain, tgt, down, lens, acc, s1, r1, s2, r2, ug, gg, st, part_s, part_r,
           ebuf, mats, projected, load_sem, rs_send, rs_recv, ag_send, ag_recv, pair_send, pair_recv):
    m = n // 2
    q = n // 8
    p = m // q
    rows, half = res.shape
    width = 2 * half
    vocab = 2 * lens.shape[1]
    span = half // chunks
    blk = span // m
    grp, me = lax.axis_index("grp"), lax.axis_index("neur")
    core = lax.rem(me, 2)
    spot = lax.rem(me // 2, q) * p + me // (2 * q)
    other = 1 - core

    def half_of(c):
        return pl.ds(pl.multiple_of(c * half, half), half)

    loads = [pltpu.make_async_copy(act_hbm, act, load_sem.at[0])]
    for slot in range(2 * chunks):
        at = (other, core)[slot // chunks] * half + (slot % chunks) * span
        cols = pl.ds(pl.multiple_of(at, span), span)
        loads.append(pltpu.make_async_copy(down_hbm.at[:, cols], down.at[:, cols], load_sem.at[1 + slot]))
    for slot, (src, dst) in enumerate(((lens_hbm.at[:, half_of(core)], lens.at[core]), (res_hbm.at[:, half_of(core)], res),
                                       (gain_hbm, rawgain), (tgt_hbm, tgt))):
        loads.append(pltpu.make_async_copy(src, dst, load_sem.at[1 + 2 * chunks + slot]))
    for load in loads:
        load.start()

    def dev(spot_at, c_at):
        return (grp, (lax.rem(spot_at, p) * q + spot_at // p) * 2 + c_at)

    core_peer = dev(spot, other)
    ahead = [lax.rem(spot + o, m) for o in range(m)]
    behind = [lax.rem(spot + m - o, m) for o in range(m)]
    barrier = pltpu.get_barrier_semaphore()
    for peer in [core_peer] + [dev(at, core) for at in ahead[1:]]:
        pl.semaphore_signal(barrier, inc=1, device_id=peer, device_id_type=MESH)

    sent = []

    def flush():
        for copy in sent:
            copy.wait_send()
        sent.clear()

    def send(src, dst, send_sem, recv_sem, peer):
        copy = pltpu.make_async_remote_copy(
            src_ref=src, dst_ref=dst, send_sem=send_sem, recv_sem=recv_sem,
            device_id=peer, device_id_type=MESH)
        copy.start()
        sent.append(copy)
        return copy


    def cols_of(c, j):
        return pl.ds(pl.multiple_of(c * span + j * blk, blk), blk)

    def send_sums(rd, c, part):
        ss, rs = rs_send.at[rd, c], rs_recv.at[rd, c]
        copies = []
        for o in range(1, m):
            s2[rd, c, o - 1] = pack(part(ahead[o]))
            copies.append(send(s2.at[rd, c, o - 1], r2.at[rd, c, o - 1], ss.at[o], rs.at[o], dev(ahead[o], core)))
        return copies

    def take_sums(rd, c, copies, total):
        for o in range(1, m):
            copies[o - 1].wait_recv()
            total = total + unpack(r2[rd, c, o - 1], rows)
        return total

    def gather(rd, c, own):
        ss, rs = ag_send.at[rd, c], ag_recv.at[rd, c]
        return [send(own, own, ss.at[o], rs.at[o], dev(ahead[o], core)) for o in range(1, m)]

    def split(x):
        high = x.astype(BF16).astype(F32)
        return jnp.concatenate([high, x - high], axis=0).astype(BF16)

    loads[0].wait()
    activations = act[...]

    def lane_sum(x):
        total = x[:, :LANES]
        for at in range(LANES, x.shape[1], LANES):
            total = total + x[:, at : at + LANES]
        return total

    def head(c):
        return lens[:, :, c * span : (c + 1) * span].reshape(vocab, span)

    def joined(buf, c, base):
        return jnp.concatenate([unpack(buf[c, base + j], rows) for j in range(m)], axis=1)

    mats[...] = jnp.zeros_like(mats)
    projected[...] = jnp.zeros_like(projected)
    acc_a, acc_b = mats.at[0], mats.at[1]
    sq_rr, sq_ru, sq_uu = (mats.at[2 + i, pl.ds(0, rows)] for i in range(3))

    def residual_terms(heads):
        for load in loads[1 + 2 * chunks :]:
            load.wait()
        heads.wait_recv()
        mine = rawgain[core].astype(F32)
        for at in range(half // LANES):
            gain[:, at * LANES : (at + 1) * LANES] = mine[at : at + 1, :]
        for c in range(chunks):
            cols = slice(c * span, (c + 1) * span)
            base = res[:, cols].astype(F32)
            sq_rr[...] += lane_sum(base * base)
            acc_a[:, :vocab] += nt(split(gain[:, cols] * base), head(c))

    with jax.named_scope("update_sum"):
        def product(c, at, j):
            cols = pl.ds(pl.multiple_of(at * half + c * span + j * blk, blk), blk)
            return jnp.dot(activations, down[:, cols], preferred_element_type=F32)

        firsts = []
        for c in range(chunks):
            loads[1 + c].wait()
            for j in range(m):
                s1[c, j] = pack(product(c, other, j))
            if c == 0:
                pl.semaphore_wait(barrier, m)
            firsts.append(send(s1.at[c], r1.at[c], pair_send.at[2 + c], pair_recv.at[2 + c], core_peer))
        heads = send(lens_hbm.at[:, half_of(other)], lens.at[core], pair_send.at[0], pair_recv.at[0], core_peer)
        for c in range(chunks):
            loads[1 + chunks + c].wait()
            for j in range(m):
                acc[c, j] = product(c, core, j)

        sums = []
        for c in range(chunks):
            firsts[c].wait_recv()

            def halved(j):
                return acc[c, j] + unpack(r1[c, j], rows)

            sums.append((send_sums(0, c, halved), halved(spot)))
        residual_terms(heads)

    with jax.named_scope("update_gather"):
        updates, gathers = [], []
        for c in range(chunks):
            updates.append(take_sums(0, c, *sums[c]))
            ug[c, spot] = pack(updates[c])
            gathers.append(gather(0, c, ug.at[c, spot]))
        for c in range(chunks):
            for copy in gathers[c]:
                copy.wait_recv()
            cols = slice(c * span, (c + 1) * span)
            up = joined(ug, c, 0)
            sq_ru[...] += lane_sum(res[:, cols].astype(F32) * up)
            sq_uu[...] += lane_sum(up * up)
            acc_b[:, :vocab] += nt(split(gain[:, cols] * up), head(c))

    with jax.named_scope("pair_sum"):
        lane = lax.broadcasted_iota(jnp.int32, (rows, LANES), 1)
        part_s[0] = acc_a[:rows, :] + acc_a[rows:, :]
        part_s[1] = acc_b[:rows, :] + acc_b[rows:, :]
        norms = jnp.zeros((rows, LANES), F32)
        for i, sq in enumerate((sq_rr, sq_ru, sq_uu)):
            norms = jnp.where(lane == i, jnp.sum(sq[...], axis=1, keepdims=True), norms)
        part_s[2] = norms
        send(part_s, part_r, pair_send.at[1], pair_recv.at[1], core_peer).wait_recv()

    with jax.named_scope("softmax_parts"):
        a_log = (part_s[0] + part_r[0])[:, :vocab]
        b_log = (part_s[1] + part_r[1])[:, :vocab]
        norms = part_s[2] + part_r[2]
        rr = norms[:, 0:1] * (1.0 / width)
        ru = norms[:, 1:2] * (2.0 / width)
        uu = norms[:, 2:3] * (1.0 / width)
        alphas = (lane + 1).astype(F32) / STEPS
        live = lane < STEPS
        inv_root = 1.0 / jnp.sqrt(rr + alphas * ru + alphas * alphas * uu + EPS)
        inv_root = jnp.where(live, inv_root, 0.0)
        square = lax.broadcasted_iota(jnp.int32, (rows, rows), 0) == lax.broadcasted_iota(jnp.int32, (rows, rows), 1)
        target = jnp.sum(jnp.where(square, tgt[...].astype(F32), 0.0), axis=1, keepdims=True).astype(jnp.int32)
        hit = lax.broadcasted_iota(jnp.int32, (rows, vocab), 1) + (me // 2) * vocab == target
        a_hit = jnp.sum(jnp.where(hit, a_log, 0.0), axis=1, keepdims=True)
        b_hit = jnp.sum(jnp.where(hit, b_log, 0.0), axis=1, keepdims=True)
        peaks = jnp.zeros((rows, LANES), F32)
        packed = jnp.where(lane == 3 * STEPS, a_hit, jnp.where(lane == 3 * STEPS + 1, b_hit, 0.0))
        for k in range(STEPS):
            logits = (a_log + ((k + 1) / STEPS) * b_log) * inv_root[:, k : k + 1]
            peak = jnp.max(logits, axis=1, keepdims=True)
            grown = jnp.exp(logits - peak)
            ebuf[k] = grown
            peaks = jnp.where(lane == k, peak, peaks)
            packed = jnp.where(lane == STEPS + k, jnp.sum(grown, axis=1, keepdims=True), packed)
            packed = jnp.where(lane == 2 * STEPS + k, jnp.sum(grown * logits, axis=1, keepdims=True), packed)
        st[spot] = fold(jnp.where(live, peaks, packed))
    with jax.named_scope("softmax_gather"):
        copies = gather(1, 0, st.at[spot])
        for copy in sent[: -len(copies)]:
            copy.wait_send()
        del sent[: -len(copies)]
        for copy in copies:
            copy.wait_recv()

    with jax.named_scope("softmax_whole"):
        top = st[0]
        for j in range(1, m):
            top = jnp.maximum(top, st[j])
        total, moment, plain = (jnp.zeros(top.shape, F32) for _ in range(3))
        for j in range(m):
            x = st[j]
            factor = jnp.exp(x - top)
            total += factor * pltpu.roll(x, LANES - STEPS, 1)
            moment += factor * pltpu.roll(x, LANES - 2 * STEPS, 1)
            plain += x
        top, total, moment, plain = unfold(top), unfold(total), unfold(moment), unfold(plain)
        total = jnp.where(live, total, 1.0)
        chosen = (plain[:, 3 * STEPS : 3 * STEPS + 1] + alphas * plain[:, 3 * STEPS + 1 : 3 * STEPS + 2]) * inv_root
        logp[...] = (chosen - top - jnp.log(total))[:, :STEPS]
        weight = (chosen - moment / total) * inv_root * inv_root * (1.0 / width)
        weight = jnp.where(live, weight, 0.0)
        first_sum = jnp.sum(weight, axis=1, keepdims=True)
        second_sum = jnp.sum(weight * alphas, axis=1, keepdims=True)
        scale = jnp.where(live, jnp.exp(peaks - top), 0.0) / total * inv_root
        coefficient = jnp.where(hit, jnp.sum(inv_root, axis=1, keepdims=True), 0.0)
        for k in range(STEPS):
            coefficient = coefficient - ebuf[k] * scale[:, k : k + 1]
        coefficient = coefficient.astype(BF16)

    with jax.named_scope("back_sum"):
        sums = []
        for c in range(chunks):
            def back_part(j):
                block = lens[:, :, cols_of(c, j)].reshape(vocab, blk)
                return jnp.dot(coefficient, block, preferred_element_type=F32)

            sums.append((send_sums(1, c, back_part), back_part(spot)))

    with jax.named_scope("gradient_gather"):
        gathers, relays = [], []

        for c in range(chunks):
            back = take_sums(1, c, *sums[c])
            own = cols_of(c, spot)
            gg[c, core * m + spot] = pack(
                gain[:, own] * back - first_sum * res[:, own].astype(F32) - second_sum * updates[c])
            gathers.append(gather(2, c, gg.at[c, core * m + spot]))

        def project(c, at):
            cols = pl.ds(pl.multiple_of(at * half + c * span, span), span)
            projected[...] += nt(joined(gg, c, at * m).astype(BF16), down[:, cols])

        for c in range(chunks):
            for copy in gathers[c]:
                copy.wait_recv()
            block = gg.at[c, pl.ds(core * m, m)]
            relays.append(send(block, block, ag_send.at[2, c, m], ag_recv.at[2, c, m], core_peer))
            project(c, core)
            if c == 0:
                flush()
            relays[c].wait_recv()
            project(c, other)
    attr[...] = 16.0 / STEPS * activations.astype(F32) * projected[...]
    flush()


def solution(mesh):
    n = mesh.shape["neur"]
    m = n // 2

    def local(activations, residual, down_weight, norm_gain, lens_weight, targets):
        rows, width = residual.shape
        neurons, vocab = down_weight.shape[0], lens_weight.shape[0]
        chunks = 2 if width // n % 512 == 0 else 1
        blk = width // n // chunks
        piece = (2 * rows, blk // 2) if blk % 256 == 0 else (rows + -rows % 16, blk)
        vmem, hbm = pl.BlockSpec(memory_space=pltpu.VMEM), pl.BlockSpec(memory_space=pltpu.HBM)
        sem = pltpu.SemaphoreType.DMA
        half = width // 2
        gains = (2, half // LANES, LANES)
        return pl.pallas_call(
            functools.partial(kernel, n, chunks),
            out_shape=(
                jax.ShapeDtypeStruct((rows, neurons), F32),
                jax.ShapeDtypeStruct((rows, STEPS), F32),
            ),
            in_specs=[hbm] * 6,
            out_specs=(vmem, vmem),
            scratch_shapes=[
                pltpu.VMEM(activations.shape, BF16),
                pltpu.VMEM((rows, half), BF16),
                pltpu.VMEM(gains, BF16),
                pltpu.VMEM((1, half), F32),
                pltpu.VMEM((1, rows), jnp.int32),
                pltpu.VMEM(down_weight.shape, BF16),
                pltpu.VMEM((2, vocab, half), BF16),
                pltpu.VMEM((chunks, m, rows, blk), F32),
                pltpu.VMEM((chunks, m) + piece, BF16),
                pltpu.VMEM((chunks, m) + piece, BF16),
                pltpu.VMEM((2, chunks, m - 1) + piece, BF16),
                pltpu.VMEM((2, chunks, m - 1) + piece, BF16),
                pltpu.VMEM((chunks, m) + piece, BF16),
                pltpu.VMEM((chunks, n) + piece, BF16),
                pltpu.VMEM((m, 16, LANES), F32),
                pltpu.VMEM((3, rows, LANES), F32),
                pltpu.VMEM((3, rows, LANES), F32),
                pltpu.VMEM((STEPS, rows, 2 * vocab), F32),
                pltpu.VMEM((5, 2 * rows, LANES), F32),
                pltpu.VMEM((rows, neurons), F32),
                sem((5 + 2 * chunks,)),
                sem((2, chunks, m)),
                sem((2, chunks, m)),
                sem((3, chunks, n)),
                sem((3, chunks, n)),
                sem((2 + chunks,)),
                sem((2 + chunks,)),
            ],
            compiler_params=pltpu.CompilerParams(
                collective_id=0, has_side_effects=True, vmem_limit_bytes=40 * 1024 * 1024
            ),
        )(*[pltpu.with_memory_space_constraint(x, pltpu.HBM) for x in (activations, residual, norm_gain.reshape(gains), targets.reshape(1, rows), down_weight, lens_weight)])

    placed = (P("grp", "neur"), P("grp", None), P("neur", None), P(), P("neur", None), P("grp"))
    return jax.shard_map(
        local,
        mesh=mesh,
        in_specs=placed,
        out_specs=(P("grp", "neur"), P("grp", None)),
        check_vma=False,
    )
```

```python
import functools

import jax
import jax.numpy as jnp
from jax import lax
from jax.experimental import pallas as pl
from jax.experimental.pallas import tpu as pltpu
from jax.sharding import PartitionSpec as P

MESH = pl.DeviceIdType.MESH
STEPS = 20
EPS = 1e-05
F32, BF16 = jnp.float32, jnp.bfloat16
LANES = 128


def nt(x, y):
    return lax.dot_general(x, y, (((1,), (1,)), ((), ())), preferred_element_type=F32)


def pack(x):
    rows, cols = x.shape
    if cols % 256 == 0:
        return jnp.concatenate([x[:, : cols // 2], x[:, cols // 2 :]], axis=0).astype(BF16)
    return jnp.concatenate([x, jnp.zeros((-rows % 16, cols), F32)], axis=0).astype(BF16)


def unpack(y, rows):
    y = y.astype(F32)
    if y.shape[0] == 2 * rows:
        return jnp.concatenate([y[:rows], y[rows:]], axis=1)
    return y[:rows]


def fold(x):
    lane = lax.broadcasted_iota(jnp.int32, (8, LANES), 1)
    first = jnp.where(lane < LANES // 2, x[:8], pltpu.roll(x[8:16], LANES // 2, 1))
    return jnp.concatenate([first, x[16:24]], axis=0)


def unfold(y):
    return jnp.concatenate([y[:8], pltpu.roll(y[:8], LANES // 2, 1), y[8:16]], axis=0)


def kernel(n, chunks, act_hbm, res_hbm, gain_hbm, tgt_hbm, down_hbm, lens_hbm, attr, logp,
           act, res, rawgain, gain, tgt, down, lens, acc, s1, r1, s2, r2, ug, gg, st, part_s, part_r,
           ebuf, mats, scores, projected, load_sem, rs_send, rs_recv, ag_send, ag_recv, pair_send, pair_recv):
    m = n // 2
    q = n // 8
    p = m // q
    rows, half = res.shape
    width = 2 * half
    vocab = 2 * lens.shape[1]
    span = half // chunks
    blk = span // m
    grp, me = lax.axis_index("grp"), lax.axis_index("neur")
    core = lax.rem(me, 2)
    spot = lax.rem(me // 2, q) * p + me // (2 * q)
    other = 1 - core

    def half_of(c):
        return pl.ds(pl.multiple_of(c * half, half), half)

    loads = [pltpu.make_async_copy(act_hbm, act, load_sem.at[0])]
    for slot in range(2 * chunks):
        at = (other, core)[slot // chunks] * half + (slot % chunks) * span
        cols = pl.ds(pl.multiple_of(at, span), span)
        loads.append(pltpu.make_async_copy(down_hbm.at[:, cols], down.at[:, cols], load_sem.at[1 + slot]))
    for slot, (src, dst) in enumerate(((lens_hbm.at[:, half_of(core)], lens.at[core]), (res_hbm.at[:, half_of(core)], res),
                                       (gain_hbm, rawgain), (tgt_hbm, tgt))):
        loads.append(pltpu.make_async_copy(src, dst, load_sem.at[1 + 2 * chunks + slot]))
    for load in loads:
        load.start()

    def dev(spot_at, c_at):
        return (grp, (lax.rem(spot_at, p) * q + spot_at // p) * 2 + c_at)

    core_peer = dev(spot, other)
    ahead = [lax.rem(spot + o, m) for o in range(m)]
    behind = [lax.rem(spot + m - o, m) for o in range(m)]
    barrier = pltpu.get_barrier_semaphore()
    for peer in [core_peer] + [dev(at, core) for at in ahead[1:]]:
        pl.semaphore_signal(barrier, inc=1, device_id=peer, device_id_type=MESH)

    sent = []

    def flush():
        for copy in sent:
            copy.wait_send()
        sent.clear()

    def send(src, dst, send_sem, recv_sem, peer):
        copy = pltpu.make_async_remote_copy(
            src_ref=src, dst_ref=dst, send_sem=send_sem, recv_sem=recv_sem,
            device_id=peer, device_id_type=MESH)
        copy.start()
        sent.append(copy)
        return copy


    def cols_of(c, j):
        return pl.ds(pl.multiple_of(c * span + j * blk, blk), blk)

    def send_sums(rd, c, part):
        ss, rs = rs_send.at[rd, c], rs_recv.at[rd, c]
        copies = []
        for o in range(1, m):
            s2[rd, c, o - 1] = pack(part(ahead[o]))
            copies.append(send(s2.at[rd, c, o - 1], r2.at[rd, c, o - 1], ss.at[o], rs.at[o], dev(ahead[o], core)))
        return copies

    def take_sums(rd, c, copies, total):
        for o in range(1, m):
            copies[o - 1].wait_recv()
            total = total + unpack(r2[rd, c, o - 1], rows)
        return total

    def gather(rd, c, own):
        ss, rs = ag_send.at[rd, c], ag_recv.at[rd, c]
        return [send(own, own, ss.at[o], rs.at[o], dev(ahead[o], core)) for o in range(1, m)]

    def split(x):
        high = x.astype(BF16).astype(F32)
        return jnp.concatenate([high, x - high], axis=0).astype(BF16)

    loads[0].wait()
    activations = act[...]

    def lane_sum(x):
        total = x[:, :LANES]
        for at in range(LANES, x.shape[1], LANES):
            total = total + x[:, at : at + LANES]
        return total

    def head(c):
        return lens[:, :, c * span : (c + 1) * span].reshape(vocab, span)

    def joined(buf, c, base):
        return jnp.concatenate([unpack(buf[c, base + j], rows) for j in range(m)], axis=1)

    mats[...] = jnp.zeros_like(mats)
    projected[...] = jnp.zeros_like(projected)
    scores[...] = jnp.zeros_like(scores)
    sq_rr, sq_ru, sq_uu = (mats.at[2 + i, pl.ds(0, rows)] for i in range(3))

    def residual_terms(heads):
        for load in loads[1 + 2 * chunks :]:
            load.wait()
        heads.wait_recv()
        mine = rawgain[core].astype(F32)
        for at in range(half // LANES):
            gain[:, at * LANES : (at + 1) * LANES] = mine[at : at + 1, :]
        for c in range(chunks):
            cols = slice(c * span, (c + 1) * span)
            base = res[:, cols].astype(F32)
            sq_rr[...] += lane_sum(base * base)
            scores[0, :, : 2 * rows] += nt(head(c), split(gain[:, cols] * base))

    with jax.named_scope("update_sum"):
        def product(c, at, j):
            cols = pl.ds(pl.multiple_of(at * half + c * span + j * blk, blk), blk)
            return jnp.dot(activations, down[:, cols], preferred_element_type=F32)

        firsts = []
        for c in range(chunks):
            loads[1 + c].wait()
            for j in range(m):
                s1[c, j] = pack(product(c, other, j))
            if c == 0:
                pl.semaphore_wait(barrier, m)
            firsts.append(send(s1.at[c], r1.at[c], pair_send.at[2 + c], pair_recv.at[2 + c], core_peer))
        heads = send(lens_hbm.at[:, half_of(other)], lens.at[core], pair_send.at[0], pair_recv.at[0], core_peer)
        for c in range(chunks):
            loads[1 + chunks + c].wait()
            for j in range(m):
                acc[c, j] = product(c, core, j)

        sums = []
        for c in range(chunks):
            firsts[c].wait_recv()

            def halved(j):
                return acc[c, j] + unpack(r1[c, j], rows)

            sums.append((send_sums(0, c, halved), halved(spot)))
        residual_terms(heads)

    with jax.named_scope("update_gather"):
        updates, gathers = [], []
        for c in range(chunks):
            updates.append(take_sums(0, c, *sums[c]))
            ug[c, spot] = pack(updates[c])
            gathers.append(gather(0, c, ug.at[c, spot]))
        for c in range(chunks):
            for copy in gathers[c]:
                copy.wait_recv()
            cols = slice(c * span, (c + 1) * span)
            up = joined(ug, c, 0)
            sq_ru[...] += lane_sum(res[:, cols].astype(F32) * up)
            sq_uu[...] += lane_sum(up * up)
            scores[1, :, : 2 * rows] += nt(head(c), split(gain[:, cols] * up))

    with jax.named_scope("pair_sum"):
        lane = lax.broadcasted_iota(jnp.int32, (rows, LANES), 1)
        for i in range(2):
            turned = scores[i].T
            part_s[i] = turned[:rows] + turned[rows : 2 * rows]
        norms = jnp.zeros((rows, LANES), F32)
        for i, sq in enumerate((sq_rr, sq_ru, sq_uu)):
            norms = jnp.where(lane == i, jnp.sum(sq[...], axis=1, keepdims=True), norms)
        part_s[2] = norms
        send(part_s, part_r, pair_send.at[1], pair_recv.at[1], core_peer).wait_recv()

    with jax.named_scope("softmax_parts"):
        a_log = (part_s[0] + part_r[0])[:, :vocab]
        b_log = (part_s[1] + part_r[1])[:, :vocab]
        norms = part_s[2] + part_r[2]
        rr = norms[:, 0:1] * (1.0 / width)
        ru = norms[:, 1:2] * (2.0 / width)
        uu = norms[:, 2:3] * (1.0 / width)
        alphas = (lane + 1).astype(F32) / STEPS
        live = lane < STEPS
        inv_root = 1.0 / jnp.sqrt(rr + alphas * ru + alphas * alphas * uu + EPS)
        inv_root = jnp.where(live, inv_root, 0.0)
        square = lax.broadcasted_iota(jnp.int32, (rows, rows), 0) == lax.broadcasted_iota(jnp.int32, (rows, rows), 1)
        target = jnp.sum(jnp.where(square, tgt[...].astype(F32), 0.0), axis=1, keepdims=True).astype(jnp.int32)
        hit = lax.broadcasted_iota(jnp.int32, (rows, vocab), 1) + (me // 2) * vocab == target
        a_hit = jnp.sum(jnp.where(hit, a_log, 0.0), axis=1, keepdims=True)
        b_hit = jnp.sum(jnp.where(hit, b_log, 0.0), axis=1, keepdims=True)
        peaks = jnp.zeros((rows, LANES), F32)
        packed = jnp.where(lane == 3 * STEPS, a_hit, jnp.where(lane == 3 * STEPS + 1, b_hit, 0.0))
        for k in range(STEPS):
            logits = (a_log + ((k + 1) / STEPS) * b_log) * inv_root[:, k : k + 1]
            peak = jnp.max(logits, axis=1, keepdims=True)
            grown = jnp.exp(logits - peak)
            ebuf[k] = grown
            peaks = jnp.where(lane == k, peak, peaks)
            packed = jnp.where(lane == STEPS + k, jnp.sum(grown, axis=1, keepdims=True), packed)
            packed = jnp.where(lane == 2 * STEPS + k, jnp.sum(grown * logits, axis=1, keepdims=True), packed)
        st[spot] = fold(jnp.where(live, peaks, packed))
    with jax.named_scope("softmax_gather"):
        copies = gather(1, 0, st.at[spot])
        for copy in sent[: -len(copies)]:
            copy.wait_send()
        del sent[: -len(copies)]
        for copy in copies:
            copy.wait_recv()

    with jax.named_scope("softmax_whole"):
        top = st[0]
        for j in range(1, m):
            top = jnp.maximum(top, st[j])
        total, moment, plain = (jnp.zeros(top.shape, F32) for _ in range(3))
        for j in range(m):
            x = st[j]
            factor = jnp.exp(x - top)
            total += factor * pltpu.roll(x, LANES - STEPS, 1)
            moment += factor * pltpu.roll(x, LANES - 2 * STEPS, 1)
            plain += x
        top, total, moment, plain = unfold(top), unfold(total), unfold(moment), unfold(plain)
        total = jnp.where(live, total, 1.0)
        chosen = (plain[:, 3 * STEPS : 3 * STEPS + 1] + alphas * plain[:, 3 * STEPS + 1 : 3 * STEPS + 2]) * inv_root
        logp[...] = (chosen - top - jnp.log(total))[:, :STEPS]
        weight = (chosen - moment / total) * inv_root * inv_root * (1.0 / width)
        weight = jnp.where(live, weight, 0.0)
        first_sum = jnp.sum(weight, axis=1, keepdims=True)
        second_sum = jnp.sum(weight * alphas, axis=1, keepdims=True)
        scale = jnp.where(live, jnp.exp(peaks - top), 0.0) / total * inv_root
        coefficient = jnp.where(hit, jnp.sum(inv_root, axis=1, keepdims=True), 0.0)
        for k in range(STEPS):
            coefficient = coefficient - ebuf[k] * scale[:, k : k + 1]
        coefficient = coefficient.astype(BF16)

    with jax.named_scope("back_sum"):
        sums = []
        for c in range(chunks):
            def back_part(j):
                block = lens[:, :, cols_of(c, j)].reshape(vocab, blk)
                return jnp.dot(coefficient, block, preferred_element_type=F32)

            sums.append((send_sums(1, c, back_part), back_part(spot)))

    with jax.named_scope("gradient_gather"):
        gathers, relays = [], []

        for c in range(chunks):
            back = take_sums(1, c, *sums[c])
            own = cols_of(c, spot)
            gg[c, core * m + spot] = pack(
                gain[:, own] * back - first_sum * res[:, own].astype(F32) - second_sum * updates[c])
            gathers.append(gather(2, c, gg.at[c, core * m + spot]))

        def project(c, at):
            cols = pl.ds(pl.multiple_of(at * half + c * span, span), span)
            projected[: down.shape[0], :rows] += nt(down[:, cols], joined(gg, c, at * m).astype(BF16))

        for c in range(chunks):
            for copy in gathers[c]:
                copy.wait_recv()
            block = gg.at[c, pl.ds(core * m, m)]
            relays.append(send(block, block, ag_send.at[2, c, m], ag_recv.at[2, c, m], core_peer))
            project(c, core)
            if c == 0:
                flush()
            relays[c].wait_recv()
            project(c, other)
    attr[...] = 16.0 / STEPS * activations.astype(F32) * projected[...].T[:rows, : down.shape[0]]
    flush()


def solution(mesh):
    n = mesh.shape["neur"]
    m = n // 2

    def local(activations, residual, down_weight, norm_gain, lens_weight, targets):
        rows, width = residual.shape
        neurons, vocab = down_weight.shape[0], lens_weight.shape[0]
        chunks = 2 if width // n % 512 == 0 else 1
        blk = width // n // chunks
        piece = (2 * rows, blk // 2) if blk % 256 == 0 else (rows + -rows % 16, blk)
        vmem, hbm = pl.BlockSpec(memory_space=pltpu.VMEM), pl.BlockSpec(memory_space=pltpu.HBM)
        sem = pltpu.SemaphoreType.DMA
        half = width // 2
        gains = (2, half // LANES, LANES)
        return pl.pallas_call(
            functools.partial(kernel, n, chunks),
            out_shape=(
                jax.ShapeDtypeStruct((rows, neurons), F32),
                jax.ShapeDtypeStruct((rows, STEPS), F32),
            ),
            in_specs=[hbm] * 6,
            out_specs=(vmem, vmem),
            scratch_shapes=[
                pltpu.VMEM(activations.shape, BF16),
                pltpu.VMEM((rows, half), BF16),
                pltpu.VMEM(gains, BF16),
                pltpu.VMEM((1, half), F32),
                pltpu.VMEM((1, rows), jnp.int32),
                pltpu.VMEM(down_weight.shape, BF16),
                pltpu.VMEM((2, vocab, half), BF16),
                pltpu.VMEM((chunks, m, rows, blk), F32),
                pltpu.VMEM((chunks, m) + piece, BF16),
                pltpu.VMEM((chunks, m) + piece, BF16),
                pltpu.VMEM((2, chunks, m - 1) + piece, BF16),
                pltpu.VMEM((2, chunks, m - 1) + piece, BF16),
                pltpu.VMEM((chunks, m) + piece, BF16),
                pltpu.VMEM((chunks, n) + piece, BF16),
                pltpu.VMEM((m, 16, LANES), F32),
                pltpu.VMEM((3, rows, LANES), F32),
                pltpu.VMEM((3, rows, LANES), F32),
                pltpu.VMEM((STEPS, rows, 2 * vocab), F32),
                pltpu.VMEM((5, 2 * rows, LANES), F32),
                pltpu.VMEM((2, 2 * vocab, LANES), F32),
                pltpu.VMEM((neurons + -neurons % LANES, LANES), F32),
                sem((5 + 2 * chunks,)),
                sem((2, chunks, m)),
                sem((2, chunks, m)),
                sem((3, chunks, n)),
                sem((3, chunks, n)),
                sem((2 + chunks,)),
                sem((2 + chunks,)),
            ],
            compiler_params=pltpu.CompilerParams(
                collective_id=0, has_side_effects=True, vmem_limit_bytes=40 * 1024 * 1024
            ),
        )(*[pltpu.with_memory_space_constraint(x, pltpu.HBM) for x in (activations, residual, norm_gain.reshape(gains), targets.reshape(1, rows), down_weight, lens_weight)])

    placed = (P("grp", "neur"), P("grp", None), P("neur", None), P(), P("neur", None), P("grp"))
    return jax.shard_map(
        local,
        mesh=mesh,
        in_specs=placed,
        out_specs=(P("grp", "neur"), P("grp", None)),
        check_vma=False,
    )
```
